32 devices in a mesh: fsdp: 2 (over x), ctx: 4 (over y, core), tp: 4 (over z).
Axes of the slice: x: 2, y: 2, z: 4, core: 2. Of those that a mesh axis runs over, the one named last changes fastest.
Arguments:
- tokens: bfloat16 [2, 2048, 1024], P('fsdp', 'ctx'), may hold values from -6 to 6
- segment_ids: int32 [2, 2048], P('fsdp', 'ctx'), may hold values from 0 to 2, as said below
- routes: int32 [2, 2048, 8], P('fsdp', 'ctx'), may hold values from 0 to 31, all different within a row; in each aligned block of 512 rows (0 to 511, 512 to 1023, ..., all dimensions but the last counted through in order) at most 256 rows name the same one
- gain_first: bfloat16 [1024], P(('fsdp', 'ctx')), may hold values from 0.5 to 1.5
- query_weight: bfloat16 [1024, 1024], P(('fsdp', 'ctx'), 'tp'), may hold values from -0.25 to 0.25
- key_weight: bfloat16 [1024, 512], P(('fsdp', 'ctx'), 'tp'), may hold values from -0.25 to 0.25
- value_weight: bfloat16 [1024, 512], P(('fsdp', 'ctx'), 'tp'), may hold values from -0.1875 to 0.1875
- out_weight: bfloat16 [1024, 1024], P(('fsdp', 'ctx'), 'tp'), may hold values from -1.5 to 1.5
- gain_second: bfloat16 [1024], P(('fsdp', 'ctx')), may hold values from 0.5 to 1.5
- router_weight: bfloat16 [1024, 32], P(('fsdp', 'ctx')), may hold values from -0.09375 to 0.09375
- gate_weight: bfloat16 [32, 1024, 512], P(None, ('fsdp', 'ctx'), 'tp'), may hold values from -0.1875 to 0.1875
- up_weight: bfloat16 [32, 1024, 512], P(None, ('fsdp', 'ctx'), 'tp'), may hold values from -0.1875 to 0.1875
- down_weight: bfloat16 [32, 1024, 512], P(None, ('fsdp', 'ctx'), 'tp'), may hold values from -1 to 1
- cotangent: bfloat16 [2, 2048, 1024], P('fsdp', 'ctx'), may hold values from -6 to 6
Outputs:
- output: bfloat16 [2, 2048, 1024], P('fsdp', 'ctx')
- input_grad: float32 [2, 2048, 1024], P('fsdp', 'ctx')
- first_grad: float32 [1024], P(('fsdp', 'ctx'))
- query_grad: float32 [1024, 1024], P(('fsdp', 'ctx'), 'tp')
- key_grad: float32 [1024, 512], P(('fsdp', 'ctx'), 'tp')
- value_grad: float32 [1024, 512], P(('fsdp', 'ctx'), 'tp')
- out_grad: float32 [1024, 1024], P(('fsdp', 'ctx'), 'tp')
- second_grad: float32 [1024], P(('fsdp', 'ctx'))
- router_grad: float32 [1024, 32], P(('fsdp', 'ctx'))
- gate_grad: float32 [32, 1024, 512], P(None, ('fsdp', 'ctx'), 'tp')
- up_grad: float32 [32, 1024, 512], P(None, ('fsdp', 'ctx'), 'tp')
- down_grad: float32 [32, 1024, 512], P(None, ('fsdp', 'ctx'), 'tp')
The draws below stay inside these ranges and needn't reach their ends.
Inputs may be any that keep to these rules, and one draw needn't show every extreme that they name: `segment_ids`: never falls along a sequence; each sequence holds three documents, the middle one starting within the first 256 positions and ending within the last 256. Within a token the routes differ. In each aligned block of 512 rows (one sequence's positions on one index of ctx) no expert is named by more than 256 rows, and some block reaches 256.
All inputs are finite; a program needn't handle non-finite values.
Results may differ from the reference program's by a relative error of at most 0.018.
Values may be sent and summed in bfloat16 or wider, within the bound.
No kernel may reach another device: no remote copies, remote signals or barrier semaphores. Data moves between devices by JAX's collectives and lax.ppermute only.
A program may use at most 320 MiB of HBM per device.

```python
import math
import jax
import jax.numpy as jnp
import numpy as np
from jax import lax

D = 1024
H = 16
KV = 8
HD = 64
FF = 512
EXPERTS = 32
TOP = 8
LEN = 2048
SEQS = 2
LSH = 512
CAP = 256
N_CTX = 4


def draw_segment_ids(key, part):
    key = jax.random.fold_in(key, 7)
    first_key, last_key = jax.random.split(key)
    margin = LEN // 8
    first_end = jax.random.randint(first_key, (SEQS, 1), 1, margin + 1)
    last_start = LEN - jax.random.randint(last_key, (SEQS, 1), 1, margin + 1)
    positions = jnp.arange(LEN, dtype=jnp.int32)[None, :]
    return (positions >= first_end).astype(jnp.int32) + (positions >= last_start).astype(jnp.int32)


def levels(rng, dims, cuts, low, largest):
    factor_of, own = 1.0, jax.random.fold_in(rng, 6)
    for dim, parts in cuts:
        draws = jnp.exp(jax.random.uniform(jax.random.fold_in(own, dim), (parts,), jnp.float32, low / len(cuts), largest / len(cuts)))
        factor_of = factor_of * jnp.repeat(draws, dims[dim] // parts).reshape([-1 if axis == dim else 1 for axis in range(len(dims))])
    return factor_of


def routed_block(stream_key, own, number, rows, number_of, top, bound, lean):
    order = jax.random.permutation(stream_key, number_of)
    packed, ordinary = shares(number_of, rows * top, bound, lean, True), shares(number_of, rows * top, bound, lean, False)
    places = jnp.arange(number_of)

    def named(lengths, turn):
        used = int((lengths > 0).sum())
        fixed = max(1, used // 4)
        passed = fixed + (places - fixed + turn * (used - fixed)) % max(1, number_of - fixed)
        return jnp.zeros((number_of,), jnp.int32).at[order[jnp.where(places < fixed, places, passed)]].set(jnp.asarray(lengths, jnp.int32))

    lengths = jnp.where(number % 4 == 0, named(packed, number // 4), named(ordinary, number - number // 4 - 1))
    mixed = jax.random.permutation(jax.random.fold_in(own, 3), number_of)
    source_of, sink = mixed[0:number_of // 2 * 2:2], mixed[1:number_of // 2 * 2:2]
    slack = jnp.minimum(lengths[source_of] - 1, bound - lengths[sink]) // 2
    slack = jnp.where((source_of == order[0]) | (sink == order[0]) | (lengths[sink] == 0), 0, jnp.maximum(slack, 0))
    passed = jax.random.randint(jax.random.fold_in(own, 4), (number_of // 2,), 0, 1 << 20) % (slack + 1)
    lengths = lengths.at[source_of].add(-passed).at[sink].add(passed)
    labels = jnp.searchsorted(jnp.cumsum(lengths), jnp.arange(rows * top), side="right").astype(jnp.int32)
    listing = labels.reshape(top, rows).T
    listing = listing[jax.random.permutation(jax.random.fold_in(own, 1), rows)]
    turn = jax.random.randint(jax.random.fold_in(own, 2), (rows, 1), 0, top)
    return jnp.take_along_axis(listing, (jnp.arange(top)[None, :] + turn) % top, axis=1)


def shares(amount, total, most, slope, full):
    weights = [(1 << 20) // math.isqrt(standing ** slope) + 1 for standing in range(1, amount + 1)]
    largest = most if full else min(most, max(-(-total // amount), total * weights[0] // sum(weights)))
    least = 1 if total - largest >= amount - 1 else 0
    given, rest = [largest] + [least] * (amount - 1), total - largest - least * (amount - 1)
    while rest > 0:
        free = [i for i in range(1, amount) if given[i] < largest] or [i for i in range(1, amount) if given[i] < most]
        mass, budget = sum([weights[i] for i in free]), rest
        for i in free:
            extra = min(most - given[i], max(1, budget * weights[i] // mass), rest)
            given[i] = given[i] + extra
            rest = rest - extra
    return np.array(given)


def bell_draw(own_key, shape, spread, bound, cuts=(), kind=jnp.bfloat16):
    level = levels(own_key, shape, cuts, -0.22, 0.18) if cuts else 1.0
    values = jax.random.normal(own_key, shape, jnp.float32) * spread * level
    return jnp.minimum(jnp.maximum(values, -bound), bound).astype(kind)


def setup_inputs(seed: int = 0) -> dict:
    splits = jax.random.split(jax.random.key(seed), 15)
    tokens = bell_draw(splits[0], (SEQS, LEN, D), 1.0, 6.0, ((0, 2), (1, 4)))
    segment_ids = draw_segment_ids(jax.random.fold_in(splits[14], 71), 0)
    routes_keys = jax.random.split(jax.random.fold_in(splits[2], 1), SEQS * LEN // LSH)
    routes_turns = jax.random.permutation(jax.random.fold_in(splits[2], 3), SEQS * LEN // LSH)
    routes = jax.vmap(lambda own, number: routed_block(jax.random.fold_in(splits[2], 2), own, number, LSH, EXPERTS, TOP, CAP, 1))(routes_keys, routes_turns).reshape((SEQS, LEN, TOP))
    gain_first = jnp.clip(1.0 + 0.1 * jax.random.normal(splits[3], (D,), jnp.float32), 0.5, 1.5).astype(jnp.bfloat16)
    query_weight = bell_draw(splits[4], (D, H * HD), (D // 2) ** -0.5, 0.25, ((0, 8), (1, 4)))
    key_weight = bell_draw(splits[5], (D, KV * HD), (D // 2) ** -0.5, 0.25, ((0, 8), (1, 4)))
    value_weight = bell_draw(splits[6], (D, KV * HD), D ** -0.5, 0.1875, ((0, 8), (1, 4)))
    out_weight = bell_draw(splits[7], (D, H * HD), (H * HD // 64) ** -0.5, 1.5, ((0, 8), (1, 4)))
    gain_second = jnp.clip(1.0 + 0.1 * jax.random.normal(splits[8], (D,), jnp.float32), 0.5, 1.5).astype(jnp.bfloat16)
    router_weight = bell_draw(splits[9], (D, EXPERTS), (4 * D) ** -0.5, 0.09375, ((0, 8),))
    gate_weight = bell_draw(splits[10], (EXPERTS, D, FF), D ** -0.5, 0.1875, ((1, 8), (2, 4)))
    up_weight = bell_draw(splits[11], (EXPERTS, D, FF), D ** -0.5, 0.1875, ((1, 8), (2, 4)))
    down_weight = bell_draw(splits[12], (EXPERTS, D, FF), (FF // 16) ** -0.5, 1.0, ((1, 8), (2, 4)))
    cotangent = bell_draw(splits[13], (SEQS, LEN, D), 1.0, 6.0, ((0, 2), (1, 4)))
    return {"tokens": tokens, "segment_ids": segment_ids, "routes": routes, "gain_first": gain_first, "query_weight": query_weight, "key_weight": key_weight, "value_weight": value_weight, "out_weight": out_weight, "gain_second": gain_second, "router_weight": router_weight, "gate_weight": gate_weight, "up_weight": up_weight, "down_weight": down_weight, "cotangent": cotangent}


EPSILON = 1e-06
PRECISE = lax.Precision.HIGHEST

@jax.custom_vjp
def low(v):
    return lax.optimization_barrier(v.astype(jnp.bfloat16)).astype(jnp.float32)

@jax.custom_vjp
def low_back(v):
    return v

def low_keep(v):
    return (low(v), None)

def low_pass(kept, grad):
    return (grad,)

def back_keep(v):
    return (v, None)

def back_low(kept, grad):
    return (low(grad),)
low.defvjp(low_keep, low_pass)
low_back.defvjp(back_keep, back_low)

def norm_scale(values, gain):
    return values * lax.rsqrt(lax.optimization_barrier(jnp.mean(values * values, axis=-1, keepdims=True)) + EPSILON) * gain

def attend_one(queries, key_heads, value_heads, segment):
    length = queries.shape[0]
    block_rows = min(512, length)
    scaling = queries.shape[-1] ** (-0.5)
    positions = jnp.arange(length, dtype=jnp.int32)

    def one_block(block_id):
        offset = block_id * block_rows
        query_block = lax.dynamic_slice_in_dim(queries, offset, block_rows, 0)
        row_segment = lax.dynamic_slice_in_dim(segment, offset, block_rows, 0)
        row_position = offset + jnp.arange(block_rows, dtype=jnp.int32)
        scores = low_back(jnp.einsum('qhd,khd->hqk', query_block, key_heads, precision=PRECISE) * scaling)
        allowed = (row_segment[:, None] == segment[None, :]) & (row_position[:, None] >= positions[None, :])
        scores = jnp.where(allowed[None], scores, -1e+30)
        probability = low(jax.nn.softmax(scores, axis=-1))
        return jnp.einsum('hqk,khd->qhd', probability, value_heads, precision=PRECISE)
    blocks_out = lax.map(jax.checkpoint(one_block), jnp.arange(length // block_rows, dtype=jnp.int32))
    return blocks_out.reshape(queries.shape)

def forward_layer(tokens, gain_first, query_weight, key_weight, value_weight, out_weight, gain_second, router_weight, gate_weight, up_weight, down_weight, segment_ids, routes):
    sequences, length, features = tokens.shape
    flattened = tokens.reshape(-1, features)
    normed = low(norm_scale(flattened, gain_first))
    queries = low_back(low(jnp.dot(normed, query_weight, precision=PRECISE))).reshape(sequences, length, H, HD)
    key_proj = low_back(low(jnp.dot(normed, key_weight, precision=PRECISE))).reshape(sequences, length, KV, HD)
    value_proj = low_back(low(jnp.dot(normed, value_weight, precision=PRECISE))).reshape(sequences, length, KV, HD)
    key_heads = low_back(jnp.repeat(key_proj, H // KV, axis=2))
    value_heads = low_back(jnp.repeat(value_proj, H // KV, axis=2))
    attended = lax.map(lambda inputs: attend_one(inputs[0], inputs[1], inputs[2], inputs[3]), (queries, key_heads, value_heads, segment_ids))
    attended = low_back(low(attended)).reshape(-1, H * HD)
    branch = low_back(jnp.dot(attended, out_weight.T, precision=PRECISE))
    middle = flattened + branch
    normed_second = low(norm_scale(middle, gain_second))
    logits = jnp.dot(normed_second, router_weight, precision=PRECISE)
    route_rows = routes.reshape(-1, TOP)
    gate_probs = jax.nn.softmax(jnp.take_along_axis(logits, route_rows, axis=1), axis=-1)
    flat_routes = route_rows.reshape(-1)
    pair_count = flat_routes.shape[0]
    member = (flat_routes[:, None] == jnp.arange(EXPERTS, dtype=jnp.int32)[None, :]).astype(jnp.int32)
    counts = lax.optimization_barrier(jnp.sum(member, axis=0)).astype(jnp.int32)
    starts = (jnp.cumsum(counts) - counts).astype(jnp.int32)
    sorted_ids = jnp.argsort(flat_routes, stable=True).astype(jnp.int32)
    capacity = sequences * N_CTX * CAP
    slot_ids = jnp.arange(capacity, dtype=jnp.int32)
    flat_gates = gate_probs.reshape(-1)

    def one_expert(expert_sum, inputs):
        expert_id, gate_matrix, up_matrix, down_matrix = inputs
        filled = slot_ids < counts[expert_id]
        pair_ids = sorted_ids[jnp.minimum(starts[expert_id] + slot_ids, pair_count - 1)]
        token_ids = pair_ids // TOP
        expert_rows = normed_second[token_ids]
        gate_pre = low_back(jnp.dot(expert_rows, gate_matrix, precision=PRECISE))
        up_pre = low_back(jnp.dot(expert_rows, up_matrix, precision=PRECISE))
        hidden = low(jax.nn.silu(gate_pre) * up_pre)
        result = low_back(jnp.dot(hidden, down_matrix.T, precision=PRECISE))
        slot_gate = jnp.where(filled, flat_gates[pair_ids], 0.0)
        return (expert_sum.at[token_ids].add(slot_gate[:, None] * result), None)
    expert_sum = lax.scan(jax.checkpoint(one_expert), jnp.zeros_like(flattened), (jnp.arange(EXPERTS, dtype=jnp.int32), gate_weight, up_weight, down_weight))[0]
    return (middle + expert_sum).reshape(tokens.shape)

def reference(tokens, segment_ids, routes, gain_first, query_weight, key_weight, value_weight, out_weight, gain_second, router_weight, gate_weight, up_weight, down_weight, cotangent):
    floats = tuple((array_in.astype(jnp.float32) for array_in in (tokens, gain_first, query_weight, key_weight, value_weight, out_weight, gain_second, router_weight, gate_weight, up_weight, down_weight)))

    def forward(*arrays):
        return forward_layer(*arrays, segment_ids, routes)
    output, pullback = jax.vjp(forward, *floats)
    gradients = pullback(cotangent.astype(jnp.float32))
    return (output.astype(jnp.bfloat16), gradients[0], gradients[1], gradients[2], gradients[3], gradients[4], gradients[5], gradients[6], gradients[7], gradients[8], gradients[9], gradients[10])
```

```python
import functools

import jax
import jax.numpy as jnp
from jax import lax
from jax.experimental import pallas as pl
from jax.experimental.layout import Layout, with_layout_constraint
from jax.experimental.pallas import tpu as pltpu
from jax.sharding import PartitionSpec as P

HD = 64
EXPERTS = 32
EPSILON = 1e-06
CHUNKS = 2
STEP = 4
QB = 256
F32 = jnp.float32
BF16 = jnp.bfloat16
PLANE = ("fsdp", "ctx")
ANY = pl.BlockSpec(memory_space=pl.ANY)
VMEM = pl.BlockSpec(memory_space=pltpu.VMEM)


def mm(a, b):
    return jnp.dot(a, b, preferred_element_type=F32)


def mm_nt(a, b):
    return lax.dot_general(a, b, (((1,), (1,)), ((), ())), preferred_element_type=F32)


def mm_tn(a, b):
    return lax.dot_general(a, b, (((0,), (0,)), ((), ())), preferred_element_type=F32)


def masked_scores(keys, query_t, starts, first_query, rows, scaling):
    scores = mm(keys, query_t) * scaling
    key_at = lax.broadcasted_iota(jnp.int32, (rows, QB), 0)
    query_at = first_query + lax.broadcasted_iota(jnp.int32, (rows, QB), 1)
    allowed = (key_at >= starts) & (key_at <= query_at)
    return scores, allowed


def attend_kernel(packet_ref, starts_ref, out_ref, lse_ref, keys_s, values_t_s):
    parts, _, width = packet_ref.shape
    for p in range(parts):
        keys_s[p * width : (p + 1) * width, :] = packet_ref[p, HD : 2 * HD, :].T
        values_t_s[:, p * width : (p + 1) * width] = packet_ref[p, 2 * HD : 3 * HD, :]
    scaling = HD ** (-0.5)
    for i in range(parts * width // QB):
        p, at, rows = i * QB // width, i * QB % width, (i + 1) * QB
        scores, allowed = masked_scores(
            keys_s[:rows, :],
            packet_ref[p, :HD, at : at + QB],
            starts_ref[:, i * QB : rows],
            i * QB,
            rows,
            scaling,
        )
        scores = jnp.where(allowed, scores, -1e30)
        maxima = jnp.max(scores, axis=0, keepdims=True)
        powers = jnp.exp(scores - maxima)
        totals = jnp.sum(powers, axis=0, keepdims=True)
        result = mm(values_t_s[:, :rows], powers.astype(BF16)) / totals
        out_ref[p, :, at : at + QB] = result.astype(BF16)
        lse_ref[:, i * QB : rows] = maxima + jnp.log(totals)


def attend(packet, starts):
    parts, _, width = packet.shape
    length = parts * width
    return pl.pallas_call(
        attend_kernel,
        out_shape=(
            jax.ShapeDtypeStruct((parts, HD, width), BF16),
            jax.ShapeDtypeStruct((1, length), F32),
        ),
        scratch_shapes=[pltpu.VMEM((length, HD), BF16), pltpu.VMEM((HD, length), BF16)],
        compiler_params=pltpu.CompilerParams(vmem_limit_bytes=40 << 20),
        cost_estimate=pl.CostEstimate(
            flops=2 * length * length * HD, bytes_accessed=4 * length * HD * 2, transcendentals=length * length // 2
        ),
        name="attend",
    )(packet, starts)


def attend_back_kernel(
    packet_ref, grad_ref, starts_ref, lse_ref, token_ref, out_ref, query_s, keys_s, values_s, grad_s, keys_t_s, gk_s, gv_s
):
    parts, _, width = packet_ref.shape
    for p in range(parts):
        rows = slice(p * width, (p + 1) * width)
        query_s[rows, :] = packet_ref[p, :HD, :].T
        keys_s[rows, :] = packet_ref[p, HD : 2 * HD, :].T
        values_s[rows, :] = packet_ref[p, 2 * HD : 3 * HD, :].T
        grad_s[rows, :] = grad_ref[p].T
        keys_t_s[:, rows] = packet_ref[p, HD : 2 * HD, :]
    gk_s[...] = jnp.zeros_like(gk_s)
    gv_s[...] = jnp.zeros_like(gv_s)
    scaling = HD ** (-0.5)
    for i in range(parts * width // QB):
        p, at, rows = i * QB // width, i * QB % width, (i + 1) * QB
        scores, allowed = masked_scores(
            keys_s[:rows, :],
            packet_ref[p, :HD, at : at + QB],
            starts_ref[:, i * QB : rows],
            i * QB,
            rows,
            scaling,
        )
        probs = jnp.where(allowed, jnp.exp(jnp.where(allowed, scores, -1e30) - lse_ref[:, i * QB : rows]), 0.0)
        grad_probs = mm(values_s[:rows, :], grad_ref[p, :, at : at + QB])
        inner = jnp.sum(probs * grad_probs, axis=0, keepdims=True)
        grad_scores = (probs * (grad_probs - inner)).astype(BF16)
        out_ref[p, :HD, at : at + QB] = (mm(keys_t_s[:, :rows], grad_scores) * scaling).astype(BF16)
        gk_s[:rows, :] += mm(grad_scores, query_s[i * QB : rows, :])
        gv_s[:rows, :] += mm(probs.astype(BF16), grad_s[i * QB : rows, :])
    for p in range(parts):
        rows = slice(p * width, (p + 1) * width)
        out_ref[p, HD : 2 * HD, :] = (gk_s[rows, :] * scaling).astype(BF16).T
        out_ref[p, 2 * HD :, :] = gv_s[rows, :].astype(BF16).T


def attend_back(packet, grads, starts, lse, token):
    parts, _, width = packet.shape
    length = parts * width
    return pl.pallas_call(
        attend_back_kernel,
        out_shape=jax.ShapeDtypeStruct((parts, 3 * HD, width), BF16),
        in_specs=[VMEM] * 4 + [ANY],
        scratch_shapes=[pltpu.VMEM((length, HD), BF16)] * 4
        + [pltpu.VMEM((HD, length), BF16)]
        + [pltpu.VMEM((length, HD), F32)] * 2,
        compiler_params=pltpu.CompilerParams(vmem_limit_bytes=48 << 20),
        cost_estimate=pl.CostEstimate(
            flops=5 * length * length * HD, bytes_accessed=8 * length * HD * 2, transcendentals=length * length // 2
        ),
        name="attend_back",
    )(packet, grads, starts, lse, token)


def experts_kernel(
    first, slots, begun, tokens, me_ref, h_ref, g_ref, gates_ref, *refs
):
    refs = refs[tokens:]
    sums_in, refs = refs[: 3 * begun], refs[3 * begun :]
    weights, refs = refs[:slots], refs[slots:]
    out_ref, ge_ref, dg_ref, uw_ref, gab_ref, wgu_s, wd_s, out_s, ge_s, dg_s = refs
    step = pl.program_id(0)
    group, _, per_step, depth, hidden = weights[0].shape

    @pl.when(step == 0)
    def _():
        for n, acc in enumerate((out_s, ge_s, dg_s)):
            acc[...] = sums_in[n][...] if begun else jnp.zeros_like(acc)

    def assemble(half):
        for k in range(slots // 2 * group):
            at = pl.ds(pl.multiple_of((me_ref[0] ^ k) * depth, depth), depth)
            for e in range(per_step):
                block = weights[half * slots // 2 + k // group].at[k % group]
                wgu_s[at, 2 * e * hidden : (2 * e + 1) * hidden] = block[0, e]
                wgu_s[at, (2 * e + 1) * hidden : (2 * e + 2) * hidden] = block[1, e]
                wd_s[at, e * hidden : (e + 1) * hidden] = block[2, e]

    @pl.when(step < pl.num_programs(0) // 2)
    def _():
        assemble(0)

    @pl.when(step >= pl.num_programs(0) // 2)
    def _():
        assemble(1)

    inner = mm(h_ref[...], wgu_s[...])
    raw = mm(g_ref[...], wd_s[...])
    gates = gates_ref[...]
    lane = lax.broadcasted_iota(jnp.int32, gates.shape, 1)
    dg = dg_s[...]
    for e in range(per_step):
        a = inner[:, 2 * e * hidden : (2 * e + 1) * hidden]
        b = inner[:, (2 * e + 1) * hidden : (2 * e + 2) * hidden]
        gu = raw[:, e * hidden : (e + 1) * hidden]
        here = lane == first + step * per_step + e
        gate = jnp.sum(jnp.where(here, gates, 0.0), axis=1, keepdims=True)
        s = jax.nn.sigmoid(a)
        silu = a * s
        u = (silu * b).astype(BF16).astype(F32)
        dg = dg + jnp.where(here, jnp.sum(u * gu, axis=1, keepdims=True), 0.0)
        gu = gu * gate
        uw_ref[:, e * hidden : (e + 1) * hidden] = (u * gate).astype(BF16)
        gab_ref[:, 2 * e * hidden : (2 * e + 1) * hidden] = (gu * b * s * (1.0 + a * (1.0 - s))).astype(BF16)
        gab_ref[:, (2 * e + 1) * hidden : (2 * e + 2) * hidden] = (gu * silu).astype(BF16)
    dg_s[...] = dg
    out_s[...] += mm_nt(uw_ref[...], wd_s[...])
    ge_s[...] += mm_nt(gab_ref[...], wgu_s[...])

    @pl.when(step == pl.num_programs(0) - 1)
    def _():
        out_ref[...] = out_s[...].astype(out_ref.dtype)
        ge_ref[...] = ge_s[...].astype(ge_ref.dtype)
        dg_ref[...] = dg_s[...]


def experts(first, me, h, g, gates, sums, weights, kind, tokens):
    group, _, count, depth, hidden = weights[0].shape
    slots = len(weights)
    count = 2 * count
    ahead = count // STEP // 2
    rows, features = h.shape
    whole = lambda shape: pl.BlockSpec(shape, lambda i, _: (0, 0))
    block = (group, 3, STEP, depth, hidden)
    early = pl.BlockSpec(block, lambda i, _: (0, 0, jnp.minimum(i, ahead - 1), 0, 0))
    late = pl.BlockSpec(block, lambda i, _: (0, 0, jnp.maximum(i - ahead, 0), 0, 0))
    kept = [whole((rows, features)), whole((rows, features)), whole((rows, EXPERTS))]
    outs = pl.pallas_call(
        functools.partial(experts_kernel, first, slots, bool(sums), len(tokens)),
        grid_spec=pltpu.PrefetchScalarGridSpec(
            num_scalar_prefetch=1,
            grid=(count // STEP,),
            in_specs=[whole((rows, features)), whole((rows, features)), whole((rows, EXPERTS))]
            + [ANY] * len(tokens)
            + kept[: len(sums)]
            + [early] * (slots // 2)
            + [late] * (slots // 2),
            out_specs=kept
            + [
                pl.BlockSpec((rows, STEP * hidden), lambda i, _: (0, i)),
                pl.BlockSpec((rows, 2 * STEP * hidden), lambda i, _: (0, i)),
            ],
            scratch_shapes=[
                pltpu.VMEM((features, 2 * STEP * hidden), BF16),
                pltpu.VMEM((features, STEP * hidden), BF16),
                pltpu.VMEM((rows, features), F32),
                pltpu.VMEM((rows, features), F32),
                pltpu.VMEM((rows, EXPERTS), F32),
            ],
        ),
        out_shape=[
            jax.ShapeDtypeStruct((rows, features), kind),
            jax.ShapeDtypeStruct((rows, features), kind),
            jax.ShapeDtypeStruct((rows, EXPERTS), F32),
            jax.ShapeDtypeStruct((rows, count * hidden), BF16),
            jax.ShapeDtypeStruct((rows, 2 * count * hidden), BF16),
        ],
        compiler_params=pltpu.CompilerParams(vmem_limit_bytes=60 << 20),
        cost_estimate=pl.CostEstimate(
            flops=12 * rows * features * hidden * count,
            bytes_accessed=6 * features * hidden * count,
            transcendentals=rows * hidden * count,
        ),
        name="experts",
    )(me, h, g, gates, *tokens, *sums, *weights)
    return outs[:3], outs[3], outs[4]


def weight_grads_kernel(order, me_ref, ht_ref, gt_ref, uw_ref, gab_ref, *refs):
    keep_ref, send_ref, ht_s, gt_s = refs[-4:]
    half, _, per_step, depth, hidden = keep_ref.shape

    @pl.when(pl.program_id(0) == 0)
    def _():
        for n in range(2 * half):
            k = order[n % half] + n // half
            at = pl.ds(pl.multiple_of((me_ref[0] ^ k) * depth, depth), depth)
            ht_s[n * depth : (n + 1) * depth, :] = ht_ref[at, :]
            gt_s[n * depth : (n + 1) * depth, :] = gt_ref[at, :]

    for e in range(per_step):
        ab = mm(ht_s[...], gab_ref[:, 2 * e * hidden : (2 * e + 2) * hidden]).astype(BF16)
        for t in range(2):
            parts = ab[:, t * hidden : (t + 1) * hidden].reshape(2, half, depth, hidden)
            keep_ref[:, t, e] = parts[0]
            send_ref[:, t, e] = parts[1]
    down = mm(gt_s[...], uw_ref[...]).astype(BF16)
    for e in range(per_step):
        parts = down[:, e * hidden : (e + 1) * hidden].reshape(2, half, depth, hidden)
        keep_ref[:, 2, e] = parts[0]
        send_ref[:, 2, e] = parts[1]


def weight_grads(me, ht, gt, uw, gab, shards, hidden, part, parts, tokens):
    features, rows = ht.shape
    count = uw.shape[1] // hidden // parts
    begin = part * count // STEP
    depth, half = features // shards, shards // 2
    whole = pl.BlockSpec((features, rows), lambda i, _: (0, 0))
    out = pl.BlockSpec((half, 3, STEP, depth, hidden), lambda i, _: (0, 0, i, 0, 0))
    shape = jax.ShapeDtypeStruct((half, 3, count, depth, hidden), BF16)
    return pl.pallas_call(
        functools.partial(weight_grads_kernel, slot_order(part % 2)),
        grid_spec=pltpu.PrefetchScalarGridSpec(
            num_scalar_prefetch=1,
            grid=(count // STEP,),
            in_specs=[
                whole,
                whole,
                pl.BlockSpec((rows, STEP * hidden), lambda i, _: (0, i + begin)),
                pl.BlockSpec((rows, 2 * STEP * hidden), lambda i, _: (0, i + begin)),
            ]
            + [ANY] * len(tokens),
            out_specs=[out, out],
            scratch_shapes=[pltpu.VMEM((features, rows), BF16)] * 2,
        ),
        out_shape=[shape, shape],
        compiler_params=pltpu.CompilerParams(vmem_limit_bytes=60 << 20),
        cost_estimate=pl.CostEstimate(
            flops=6 * rows * features * hidden * count,
            bytes_accessed=6 * (rows + features) * hidden * count,
            transcendentals=0,
        ),
        name="weight_grads",
    )(me, ht, gt, uw, gab, *tokens)


def swap(x, axis, bit):
    return lax.ppermute(x, axis, [(i, i ^ bit) for i in range(lax.axis_size(axis))])


def plane_bits(turn):
    wide = [("fsdp", 1 << b) for b in reversed(range(lax.axis_size("fsdp").bit_length() - 1))]
    near = [("ctx", 1 << b) for b in reversed(range(1, lax.axis_size("ctx").bit_length() - 1))]
    return wide + near if turn == 0 else near + wide


def join(xs, ys):
    out = lax.optimization_barrier((*xs, *ys))
    return list(out[: len(xs)]), list(out[len(xs) :])


def natural(x):
    return with_layout_constraint(x, Layout(major_to_minor=tuple(range(x.ndim))))


def place_of(axis, bit):
    return bit * lax.axis_size("ctx") if axis == "fsdp" else bit


def gather_own(x, turn):
    return [swap(x, axis, bit) for axis, bit in plane_bits(turn)]


def gather_plane(x, own, turn):
    slots = {0: x}
    for (axis, bit), first in zip(plane_bits(turn), own):
        place = place_of(axis, bit)
        slots.update({k + place: swap(v, axis, bit) if k else first for k, v in slots.items()})
    return slots


def gather_near(slots):
    slots = {**slots, **{k + 1: swap(v, "ctx", 1) for k, v in slots.items()}}
    count = len(slots)
    group = max(1, count // 8)
    return [jnp.stack([slots[j + s] for s in range(group)]) for j in range(0, count, group)]


def slot_order(turn):
    order = [0]
    for axis, bit in plane_bits(turn)[::-1]:
        place = place_of(axis, bit)
        order = order + [k + place for k in order]
    return order


def add_up(parts):
    return sum(p.astype(F32) for p in parts)


def scatter_steps(keep, send, turn):
    parts = [keep, swap(send, "ctx", 1)]
    for axis, bit in plane_bits(turn):
        half = parts[0].shape[0] // 2
        total = yield add_up([p[half:] for p in parts]).astype(BF16)
        parts = [p[:half] for p in parts] + [swap(total, axis, bit)]
    yield parts


def pack_kernel(me_ref, *refs):
    *ins, out_ref = refs
    at = 0
    for x in ins:
        out_ref[0, :, at : at + x.shape[1]] = x[...].astype(BF16)
        at += x.shape[1]


def scatter_wide(arrays, me):
    features = arrays[0].shape[0]
    shards = lax.axis_size("fsdp") * lax.axis_size("ctx")
    depth, columns = features // shards, sum(x.shape[1] for x in arrays)
    order = slot_order(0)
    slots = jnp.asarray(order + [k + 1 for k in order], jnp.int32) ^ me
    x = pl.pallas_call(
        pack_kernel,
        grid_spec=pltpu.PrefetchScalarGridSpec(
            num_scalar_prefetch=1,
            grid=(shards,),
            in_specs=[pl.BlockSpec((depth, x.shape[1]), lambda i, slots: (slots[i], 0)) for x in arrays],
            out_specs=pl.BlockSpec((1, depth, columns), lambda i, _: (i, 0, 0)),
        ),
        out_shape=jax.ShapeDtypeStruct((shards, depth, columns), BF16),
        name="pack",
    )(slots, *arrays)
    parts = [x]
    for axis, bit in [("ctx", 1)] + plane_bits(0):
        half = parts[0].shape[0] // 2
        total = add_up([p[half:] for p in parts]).astype(BF16)
        parts = [p[:half] for p in parts] + [swap(total, axis, bit)]
    return parts


def tp_shift(x, by):
    n = lax.axis_size("tp")
    return lax.ppermute(x, "tp", [(i, (i + by) % n) for i in range(n)])


def shifts_tp(x):
    return [x] + [tp_shift(x, by) for by in range(1, lax.axis_size("tp"))]


def order_tp(parts):
    n, i = lax.axis_size("tp"), lax.axis_index("tp")
    return [lax.select_n((i - j) % n, *parts) for j in range(n)]


def gather_tp(x):
    return jnp.stack(order_tp(shifts_tp(x)))


def scatter_tp(x):
    n, i = lax.axis_size("tp"), lax.axis_index("tp")
    parts = x.reshape(n, -1, x.shape[-1])
    row = lambda k: lax.dynamic_index_in_dim(parts, k % n, 0, keepdims=False)
    return [row(i)] + [tp_shift(row(i + by), by) for by in range(1, n)]


def norm_back(scaled, inverse, gain, upstream):
    weighted = upstream * gain
    gain_part = jnp.sum(upstream * scaled, axis=0)
    return inverse * (weighted - scaled * jnp.mean(weighted * scaled, axis=-1, keepdims=True)), gain_part


def local(
    tokens,
    segment_ids,
    routes,
    gain_first,
    query_weight,
    key_weight,
    value_weight,
    out_weight,
    gain_second,
    router_weight,
    gate_weight,
    up_weight,
    down_weight,
    cotangent,
):
    sequences, width, features = tokens.shape
    rows = sequences * width
    n_ctx = lax.axis_size("ctx")
    q_cols, kv_cols = query_weight.shape[1], key_weight.shape[1]
    repeat = q_cols // kv_cols

    hidden = gate_weight.shape[2]
    shards = lax.axis_size("fsdp") * n_ctx
    me = lax.axis_index("fsdp") * n_ctx + lax.axis_index("ctx")
    me_array = me.astype(jnp.int32).reshape(1)
    first_pack = jnp.concatenate(
        [query_weight, key_weight, value_weight, out_weight, router_weight, gain_first[:, None], gain_second[:, None]],
        axis=1,
    )
    first_full = lax.all_gather(first_pack, PLANE, axis=0, tiled=True)
    edges = (q_cols, q_cols + kv_cols, q_cols + 2 * kv_cols, 2 * q_cols + 2 * kv_cols)
    qkv_full = first_full[:, : edges[2]]
    out_own = first_full[:, edges[2] : edges[3]]
    router_full = first_full[:, edges[3] : -2]
    first_scale = first_full[:, -2].astype(F32)
    second_scale = first_full[:, -1].astype(F32)
    out_parts = shifts_tp(out_own)
    size = EXPERTS // CHUNKS
    packs = [
        jnp.stack([w[at : at + size // 2] for w in (gate_weight, up_weight, down_weight)])
        for at in range(0, EXPERTS, size // 2)
    ]

    own = [gather_own(packs[n], n) for n in range(2)]

    flat = natural(tokens.reshape(rows, features)).astype(F32)
    inverse_first = lax.rsqrt(jnp.mean(flat * flat, axis=-1, keepdims=True) + EPSILON)
    scaled_first = flat * inverse_first
    h1 = (scaled_first * first_scale).astype(BF16)
    qkv_t = lax.dot_general(qkv_full, h1, (((0,), (1,)), ((), ())), preferred_element_type=F32).astype(BF16)
    local_heads = q_cols // HD
    q_t = qkv_t[:q_cols].reshape(local_heads, HD, rows)
    k_t = jnp.repeat(qkv_t[q_cols : q_cols + kv_cols].reshape(-1, HD, rows), repeat, axis=0)
    v_t = jnp.repeat(qkv_t[q_cols + kv_cols :].reshape(-1, HD, rows), repeat, axis=0)
    labels = jnp.broadcast_to(segment_ids.reshape(1, 1, rows).astype(BF16), (n_ctx, 16, rows))
    packet = jnp.concatenate([q_t, k_t, v_t, labels], axis=1)
    [packet], firsts = join([packet], [own[n][0] for n in range(2)])
    packet = lax.all_to_all(packet, "ctx", 0, 0, tiled=True)
    segments = packet[:, 3 * HD, :].reshape(1, -1)
    ends = [jnp.sum((segments < k).astype(jnp.int32), axis=1, keepdims=True) for k in (1, 2)]
    starts = jnp.where(segments >= 2, ends[1], jnp.where(segments >= 1, ends[0], 0))
    result_t, lse = attend(packet, starts)
    [result_t], rest = join([result_t], [x for n in range(2) for x in own[n][1:]])
    many = len(rest) // 2
    own = [[firsts[n]] + rest[n * many : (n + 1) * many] for n in range(2)]
    attended_t = lax.all_to_all(result_t, "ctx", 0, 0, tiled=True).reshape(q_cols, rows)
    waiting = own[0] + own[1] + packs[2:] + out_parts[1:]
    [attended_t], waiting = join([attended_t], waiting)
    own, waiting = [waiting[: many + 1], waiting[many + 1 : 2 * many + 2]], waiting[2 * many + 2 :]
    packs[2:], out_parts[1:] = waiting[:2], waiting[2:]
    own += [gather_own(packs[2 + n], n) for n in range(2)]
    gathered = [gather_plane(packs[n], own[n], n) for n in range(2)]
    attended_full = lax.all_gather(attended_t, "tp", axis=0, tiled=True)
    out_full = jnp.concatenate(order_tp(out_parts), axis=1)

    def joined(x, n):
        keys = [(m, k) for m in (n, n + 1) for k in gathered[m]]
        [x], slots = join([x], [gathered[m][k] for m, k in keys])
        for (m, k), v in zip(keys, slots):
            gathered[m][k] = v
        return x

    attended_full = joined(attended_full, 0)
    [attended_full], firsts = join([attended_full], own[2] + own[3])
    own[2:] = [firsts[: many + 1], firsts[many + 1 :]]
    gathered[2:] = [gather_plane(packs[2 + n], own[2 + n], n) for n in range(2)]
    middle = flat + natural(
        lax.dot_general(attended_full, out_full, (((0,), (1,)), ((), ())), preferred_element_type=F32)
    )

    inverse_second = lax.rsqrt(jnp.mean(middle * middle, axis=-1, keepdims=True) + EPSILON)
    scaled_second = middle * inverse_second
    h2 = (scaled_second * second_scale).astype(BF16)
    route_rows = routes.reshape(rows, -1)
    member = jnp.any(route_rows[:, :, None] == jnp.arange(EXPERTS, dtype=jnp.int32)[None, None, :], axis=1)
    logits = jnp.where(member, mm(h2, router_full), -1e30)
    powers = jnp.where(member, jnp.exp(logits - jnp.max(logits, axis=1, keepdims=True)), 0.0)
    gates = powers / jnp.sum(powers, axis=1, keepdims=True)
    g = natural(cotangent.reshape(rows, features))
    h2_t, g_t = h2.T, g.T
    grads_of = functools.partial(weight_grads, me_array, h2_t, g_t, shards=shards, hidden=hidden, parts=2)
    weights = gather_near(gathered[0]) + gather_near(gathered[1])
    sums, uw0, gab0 = experts(0, me_array, h2, g, gates, (), weights, F32, ())
    uw0 = joined(uw0, 2)
    weights = gather_near(gathered[2]) + gather_near(gathered[3])
    halves = [grads_of(uw=uw0, gab=gab0, part=0, tokens=())]
    [gab0], weights = join([gab0], weights)
    halves.append(grads_of(uw=uw0, gab=gab0, part=1, tokens=[halves[0][0]]))
    (expert_sum, ge, dg), uw1, gab1 = experts(
        size, me_array, h2, g, gates, sums, weights, BF16, [keep for keep, _ in halves]
    )
    scatters = [scatter_steps(*halves[n], n) for n in range(2)]
    sends = [next(x) for x in scatters]
    sends = [x.send(y) for x, y in zip(scatters, sends)]
    folded = rows * EXPERTS // features
    both = lax.psum(jnp.concatenate([ge, dg.astype(BF16).reshape(folded, features)], axis=0), "tp")
    [both], sends = join([both], sends)
    ge = both[:rows].astype(F32)
    dg = both[rows:].reshape(rows, EXPERTS).astype(F32)
    dl = (gates * (dg - jnp.sum(gates * dg, axis=1, keepdims=True))).astype(BF16)
    router_part = mm_tn(h2, dl)
    gh2 = ge + mm_nt(dl, router_full)
    middle_part, second_part = norm_back(scaled_second, inverse_second, second_scale, gh2)
    gm = g.astype(F32) + middle_part

    gmr = gm.astype(BF16)
    out_part = lax.dot_general(gmr, attended_t, (((0,), (1,)), ((), ())), preferred_element_type=F32)
    gat_t = lax.dot_general(out_own, gmr, (((0,), (1,)), ((), ())), preferred_element_type=F32).astype(BF16)
    [gat_t], [expert_sum] = join([gat_t], [expert_sum])
    expert_parts = scatter_tp(expert_sum)
    head_grads = lax.all_to_all(gat_t.reshape(local_heads, HD, rows), "ctx", 0, 0, tiled=True)
    halves.append(grads_of(uw=uw1, gab=gab1, part=0, tokens=[gat_t]))
    packed_grads = attend_back(packet, head_grads, starts, lse, halves[2][0])
    [packed_grads], expert_parts = join([packed_grads], expert_parts)
    expert_parts = shifts_tp(add_up(expert_parts).astype(BF16))
    halves.append(grads_of(uw=uw1, gab=gab1, part=1, tokens=[packed_grads]))
    token_grads = lax.all_to_all(packed_grads, "ctx", 0, 0, tiled=True)
    scatters += [scatter_steps(*halves[2 + n], n) for n in range(2)]
    late = [next(x) for x in scatters[2:]]
    [token_grads], late = join([token_grads], late)
    sends += late
    kv_sum = jnp.sum(token_grads[:, HD:].astype(F32).reshape(-1, repeat, 2, HD, rows), axis=1).astype(BF16)
    grads_t = jnp.concatenate(
        [
            token_grads[:, :HD].reshape(q_cols, rows),
            kv_sum[:, 0].reshape(kv_cols, rows),
            kv_sum[:, 1].reshape(kv_cols, rows),
        ],
        axis=0,
    )
    qkv_part = lax.dot_general(h1, grads_t, (((0,), (1,)), ((), ())), preferred_element_type=F32)
    gh1 = lax.dot_general(grads_t, qkv_full, (((0,), (1,)), ((), ())), preferred_element_type=F32)
    first_part = jnp.sum(gh1 * scaled_first, axis=0)
    thin_part = jnp.concatenate(
        [router_part, first_part[:, None], second_part[:, None], jnp.zeros((features, 128 - EXPERTS - 2), F32)], axis=1
    )
    [gh1], expert_parts = join([gh1], expert_parts)
    output = (middle + jnp.concatenate(order_tp(expert_parts), axis=0).astype(F32)).astype(BF16).reshape(tokens.shape)
    gh1 = lax.psum(natural(gh1.astype(BF16)), "tp")
    wide = scatter_wide([qkv_part, out_part, thin_part], me)
    for n in range(len(scatters)):
        while n < 2 and not isinstance(sends[n], list):
            sends[n] = scatters[n].send(sends[n])
        if n >= 2:
            sends[n] = scatters[n].send(sends[n])
    count = len(wide)
    [gh1], rest = join([gh1], wide + sends[2:])
    wide, sends[2:] = rest[:count], rest[count:]
    gh1 = gh1.astype(F32)
    wide = add_up(wide)[0]
    first_grad = jnp.sum(gather_tp(wide[:, edges[3] + EXPERTS]), axis=0)
    for n in (2, 3):
        while not isinstance(sends[n], list):
            sends[n] = scatters[n].send(sends[n])
    gate_grad, up_grad, down_grad = (
        jnp.concatenate([add_up([x[0, t] for x in parts]) for parts in sends], axis=0) for t in range(3)
    )
    token_part, _ = norm_back(scaled_first, inverse_first, first_scale, gh1)
    input_grad = (gm + token_part).reshape(tokens.shape)
    return (
        output,
        input_grad,
        first_grad,
        wide[:, : edges[0]],
        wide[:, edges[0] : edges[1]],
        wide[:, edges[1] : edges[2]],
        wide[:, edges[2] : edges[3]],
        wide[:, edges[3] + EXPERTS + 1],
        wide[:, edges[3] : edges[3] + EXPERTS],
        gate_grad,
        up_grad,
        down_grad,
    )


def solution(mesh):
    return jax.shard_map(
        local,
        mesh=mesh,
        in_specs=(
            P("fsdp", "ctx", None),
            P("fsdp", "ctx"),
            P("fsdp", "ctx", None),
            P(PLANE),
            P(PLANE, "tp"),
            P(PLANE, "tp"),
            P(PLANE, "tp"),
            P(PLANE, "tp"),
            P(PLANE),
            P(PLANE, None),
            P(None, PLANE, "tp"),
            P(None, PLANE, "tp"),
            P(None, PLANE, "tp"),
            P("fsdp", "ctx", None),
        ),
        out_specs=(
            P("fsdp", "ctx", None),
            P("fsdp", "ctx", None),
            P(PLANE),
            P(PLANE, "tp"),
            P(PLANE, "tp"),
            P(PLANE, "tp"),
            P(PLANE, "tp"),
            P(PLANE),
            P(PLANE, None),
            P(None, PLANE, "tp"),
            P(None, PLANE, "tp"),
            P(None, PLANE, "tp"),
        ),
        check_vma=False,
    )
```

```python
import functools

import jax
import jax.numpy as jnp
from jax import lax
from jax.experimental import pallas as pl
from jax.experimental.layout import Layout, with_layout_constraint
from jax.experimental.pallas import tpu as pltpu
from jax.sharding import PartitionSpec as P

HD = 64
EXPERTS = 32
EPSILON = 1e-06
CHUNKS = 2
STEP = 4
QB = 256
F32 = jnp.float32
BF16 = jnp.bfloat16
PLANE = ("fsdp", "ctx")
ANY = pl.BlockSpec(memory_space=pl.ANY)
VMEM = pl.BlockSpec(memory_space=pltpu.VMEM)


def mm(a, b):
    return jnp.dot(a, b, preferred_element_type=F32)


def mm_nt(a, b):
    return lax.dot_general(a, b, (((1,), (1,)), ((), ())), preferred_element_type=F32)


def mm_tn(a, b):
    return lax.dot_general(a, b, (((0,), (0,)), ((), ())), preferred_element_type=F32)


def masked_scores(keys, query_t, starts, first_query, rows, scaling):
    scores = mm(keys, query_t) * scaling
    key_at = lax.broadcasted_iota(jnp.int32, (rows, QB), 0)
    query_at = first_query + lax.broadcasted_iota(jnp.int32, (rows, QB), 1)
    allowed = (key_at >= starts) & (key_at <= query_at)
    return scores, allowed


def attend_kernel(packet_ref, starts_ref, out_ref, lse_ref, keys_s, values_t_s):
    parts, _, width = packet_ref.shape
    for p in range(parts):
        keys_s[p * width : (p + 1) * width, :] = packet_ref[p, HD : 2 * HD, :].T
        values_t_s[:, p * width : (p + 1) * width] = packet_ref[p, 2 * HD : 3 * HD, :]
    scaling = HD ** (-0.5)
    for i in range(parts * width // QB):
        p, at, rows = i * QB // width, i * QB % width, (i + 1) * QB
        scores, allowed = masked_scores(
            keys_s[:rows, :],
            packet_ref[p, :HD, at : at + QB],
            starts_ref[:, i * QB : rows],
            i * QB,
            rows,
            scaling,
        )
        scores = jnp.where(allowed, scores, -1e30)
        maxima = jnp.max(scores, axis=0, keepdims=True)
        powers = jnp.exp(scores - maxima)
        totals = jnp.sum(powers, axis=0, keepdims=True)
        result = mm(values_t_s[:, :rows], powers.astype(BF16)) / totals
        out_ref[p, :, at : at + QB] = result.astype(BF16)
        lse_ref[:, i * QB : rows] = maxima + jnp.log(totals)


def attend(packet, starts):
    parts, _, width = packet.shape
    length = parts * width
    return pl.pallas_call(
        attend_kernel,
        out_shape=(
            jax.ShapeDtypeStruct((parts, HD, width), BF16),
            jax.ShapeDtypeStruct((1, length), F32),
        ),
        scratch_shapes=[pltpu.VMEM((length, HD), BF16), pltpu.VMEM((HD, length), BF16)],
        compiler_params=pltpu.CompilerParams(vmem_limit_bytes=40 << 20),
        cost_estimate=pl.CostEstimate(
            flops=2 * length * length * HD, bytes_accessed=4 * length * HD * 2, transcendentals=length * length // 2
        ),
        name="attend",
    )(packet, starts)


def attend_back_kernel(
    packet_ref, grad_ref, starts_ref, lse_ref, token_ref, out_ref, query_s, keys_s, values_s, grad_s, keys_t_s, gk_s, gv_s
):
    parts, _, width = packet_ref.shape
    for p in range(parts):
        rows = slice(p * width, (p + 1) * width)
        query_s[rows, :] = packet_ref[p, :HD, :].T
        keys_s[rows, :] = packet_ref[p, HD : 2 * HD, :].T
        values_s[rows, :] = packet_ref[p, 2 * HD : 3 * HD, :].T
        grad_s[rows, :] = grad_ref[p].T
        keys_t_s[:, rows] = packet_ref[p, HD : 2 * HD, :]
    gk_s[...] = jnp.zeros_like(gk_s)
    gv_s[...] = jnp.zeros_like(gv_s)
    scaling = HD ** (-0.5)
    for i in range(parts * width // QB):
        p, at, rows = i * QB // width, i * QB % width, (i + 1) * QB
        scores, allowed = masked_scores(
            keys_s[:rows, :],
            packet_ref[p, :HD, at : at + QB],
            starts_ref[:, i * QB : rows],
            i * QB,
            rows,
            scaling,
        )
        probs = jnp.where(allowed, jnp.exp(jnp.where(allowed, scores, -1e30) - lse_ref[:, i * QB : rows]), 0.0)
        grad_probs = mm(values_s[:rows, :], grad_ref[p, :, at : at + QB])
        inner = jnp.sum(probs * grad_probs, axis=0, keepdims=True)
        grad_scores = (probs * (grad_probs - inner)).astype(BF16)
        out_ref[p, :HD, at : at + QB] = (mm(keys_t_s[:, :rows], grad_scores) * scaling).astype(BF16)
        gk_s[:rows, :] += mm(grad_scores, query_s[i * QB : rows, :])
        gv_s[:rows, :] += mm(probs.astype(BF16), grad_s[i * QB : rows, :])
    for p in range(parts):
        rows = slice(p * width, (p + 1) * width)
        out_ref[p, HD : 2 * HD, :] = (gk_s[rows, :] * scaling).astype(BF16).T
        out_ref[p, 2 * HD :, :] = gv_s[rows, :].astype(BF16).T


def attend_back(packet, grads, starts, lse, tokens):
    parts, _, width = packet.shape
    length = parts * width
    return pl.pallas_call(
        attend_back_kernel,
        out_shape=jax.ShapeDtypeStruct((parts, 3 * HD, width), BF16),
        in_specs=[VMEM] * 4 + [ANY],
        scratch_shapes=[pltpu.VMEM((length, HD), BF16)] * 4
        + [pltpu.VMEM((HD, length), BF16)]
        + [pltpu.VMEM((length, HD), F32)] * 2,
        compiler_params=pltpu.CompilerParams(vmem_limit_bytes=48 << 20),
        cost_estimate=pl.CostEstimate(
            flops=5 * length * length * HD, bytes_accessed=8 * length * HD * 2, transcendentals=length * length // 2
        ),
        name="attend_back",
    )(packet, grads, starts, lse, *tokens)


def experts_kernel(
    first, slots, begun, tokens, me_ref, h_ref, g_ref, gates_ref, *refs
):
    refs = refs[tokens:]
    sums_in, refs = refs[: 3 * begun], refs[3 * begun :]
    weights, refs = refs[:slots], refs[slots:]
    out_ref, ge_ref, dg_ref, uw_ref, gab_ref, wgu_s, wd_s, out_s, ge_s, dg_s = refs
    step = pl.program_id(0)
    group, _, per_step, depth, hidden = weights[0].shape

    @pl.when(step == 0)
    def _():
        for n, acc in enumerate((out_s, ge_s, dg_s)):
            acc[...] = sums_in[n][...] if begun else jnp.zeros_like(acc)

    def assemble(half):
        for k in range(slots // 2 * group):
            at = pl.ds(pl.multiple_of((me_ref[0] ^ k) * depth, depth), depth)
            for e in range(per_step):
                block = weights[half * slots // 2 + k // group].at[k % group]
                wgu_s[at, 2 * e * hidden : (2 * e + 1) * hidden] = block[0, e]
                wgu_s[at, (2 * e + 1) * hidden : (2 * e + 2) * hidden] = block[1, e]
                wd_s[at, e * hidden : (e + 1) * hidden] = block[2, e]

    @pl.when(step < pl.num_programs(0) // 2)
    def _():
        assemble(0)

    @pl.when(step >= pl.num_programs(0) // 2)
    def _():
        assemble(1)

    inner = mm(h_ref[...], wgu_s[...])
    raw = mm(g_ref[...], wd_s[...])
    gates = gates_ref[...]
    lane = lax.broadcasted_iota(jnp.int32, gates.shape, 1)
    dg = dg_s[...]
    for e in range(per_step):
        a = inner[:, 2 * e * hidden : (2 * e + 1) * hidden]
        b = inner[:, (2 * e + 1) * hidden : (2 * e + 2) * hidden]
        gu = raw[:, e * hidden : (e + 1) * hidden]
        here = lane == first + step * per_step + e
        gate = jnp.sum(jnp.where(here, gates, 0.0), axis=1, keepdims=True)
        s = jax.nn.sigmoid(a)
        silu = a * s
        u = (silu * b).astype(BF16).astype(F32)
        dg = dg + jnp.where(here, jnp.sum(u * gu, axis=1, keepdims=True), 0.0)
        gu = gu * gate
        uw_ref[:, e * hidden : (e + 1) * hidden] = (u * gate).astype(BF16)
        gab_ref[:, 2 * e * hidden : (2 * e + 1) * hidden] = (gu * b * s * (1.0 + a * (1.0 - s))).astype(BF16)
        gab_ref[:, (2 * e + 1) * hidden : (2 * e + 2) * hidden] = (gu * silu).astype(BF16)
    dg_s[...] = dg
    out_s[...] += mm_nt(uw_ref[...], wd_s[...])
    ge_s[...] += mm_nt(gab_ref[...], wgu_s[...])

    @pl.when(step == pl.num_programs(0) - 1)
    def _():
        out_ref[...] = out_s[...].astype(out_ref.dtype)
        ge_ref[...] = ge_s[...].astype(ge_ref.dtype)
        dg_ref[...] = dg_s[...]


def experts(first, me, h, g, gates, sums, weights, kind, tokens):
    group, _, count, depth, hidden = weights[0].shape
    slots = len(weights)
    count = 2 * count
    ahead = count // STEP // 2
    rows, features = h.shape
    whole = lambda shape: pl.BlockSpec(shape, lambda i, _: (0, 0))
    block = (group, 3, STEP, depth, hidden)
    early = pl.BlockSpec(block, lambda i, _: (0, 0, jnp.minimum(i, ahead - 1), 0, 0))
    late = pl.BlockSpec(block, lambda i, _: (0, 0, jnp.maximum(i - ahead, 0), 0, 0))
    kept = [whole((rows, features)), whole((rows, features)), whole((rows, EXPERTS))]
    outs = pl.pallas_call(
        functools.partial(experts_kernel, first, slots, bool(sums), len(tokens)),
        grid_spec=pltpu.PrefetchScalarGridSpec(
            num_scalar_prefetch=1,
            grid=(count // STEP,),
            in_specs=[whole((rows, features)), whole((rows, features)), whole((rows, EXPERTS))]
            + [ANY] * len(tokens)
            + kept[: len(sums)]
            + [early] * (slots // 2)
            + [late] * (slots // 2),
            out_specs=kept
            + [
                pl.BlockSpec((rows, STEP * hidden), lambda i, _: (0, i)),
                pl.BlockSpec((rows, 2 * STEP * hidden), lambda i, _: (0, i)),
            ],
            scratch_shapes=[
                pltpu.VMEM((features, 2 * STEP * hidden), BF16),
                pltpu.VMEM((features, STEP * hidden), BF16),
                pltpu.VMEM((rows, features), F32),
                pltpu.VMEM((rows, features), F32),
                pltpu.VMEM((rows, EXPERTS), F32),
            ],
        ),
        out_shape=[
            jax.ShapeDtypeStruct((rows, features), kind),
            jax.ShapeDtypeStruct((rows, features), kind),
            jax.ShapeDtypeStruct((rows, EXPERTS), F32),
            jax.ShapeDtypeStruct((rows, count * hidden), BF16),
            jax.ShapeDtypeStruct((rows, 2 * count * hidden), BF16),
        ],
        compiler_params=pltpu.CompilerParams(vmem_limit_bytes=60 << 20),
        cost_estimate=pl.CostEstimate(
            flops=12 * rows * features * hidden * count,
            bytes_accessed=6 * features * hidden * count,
            transcendentals=rows * hidden * count,
        ),
        name="experts",
    )(me, h, g, gates, *tokens, *sums, *weights)
    return outs[:3], outs[3], outs[4]


def weight_grads_kernel(order, me_ref, ht_ref, gt_ref, uw_ref, gab_ref, *refs):
    keep_ref, send_ref, ht_s, gt_s = refs[-4:]
    half, _, per_step, depth, hidden = keep_ref.shape

    @pl.when(pl.program_id(0) == 0)
    def _():
        for n in range(2 * half):
            k = order[n % half] + n // half
            at = pl.ds(pl.multiple_of((me_ref[0] ^ k) * depth, depth), depth)
            ht_s[n * depth : (n + 1) * depth, :] = ht_ref[at, :]
            gt_s[n * depth : (n + 1) * depth, :] = gt_ref[at, :]

    for e in range(per_step):
        ab = mm(ht_s[...], gab_ref[:, 2 * e * hidden : (2 * e + 2) * hidden]).astype(BF16)
        for t in range(2):
            parts = ab[:, t * hidden : (t + 1) * hidden].reshape(2, half, depth, hidden)
            keep_ref[:, t, e] = parts[0]
            send_ref[:, t, e] = parts[1]
    down = mm(gt_s[...], uw_ref[...]).astype(BF16)
    for e in range(per_step):
        parts = down[:, e * hidden : (e + 1) * hidden].reshape(2, half, depth, hidden)
        keep_ref[:, 2, e] = parts[0]
        send_ref[:, 2, e] = parts[1]


def weight_grads(me, ht, gt, uw, gab, shards, hidden, part, parts, turn, tokens):
    features, rows = ht.shape
    count = uw.shape[1] // hidden // parts
    begin = part * count // STEP
    depth, half = features // shards, shards // 2
    whole = pl.BlockSpec((features, rows), lambda i, _: (0, 0))
    out = pl.BlockSpec((half, 3, STEP, depth, hidden), lambda i, _: (0, 0, i, 0, 0))
    shape = jax.ShapeDtypeStruct((half, 3, count, depth, hidden), BF16)
    return pl.pallas_call(
        functools.partial(weight_grads_kernel, slot_order(turn)),
        grid_spec=pltpu.PrefetchScalarGridSpec(
            num_scalar_prefetch=1,
            grid=(count // STEP,),
            in_specs=[
                whole,
                whole,
                pl.BlockSpec((rows, STEP * hidden), lambda i, _: (0, i + begin)),
                pl.BlockSpec((rows, 2 * STEP * hidden), lambda i, _: (0, i + begin)),
            ]
            + [ANY] * len(tokens),
            out_specs=[out, out],
            scratch_shapes=[pltpu.VMEM((features, rows), BF16)] * 2,
        ),
        out_shape=[shape, shape],
        compiler_params=pltpu.CompilerParams(vmem_limit_bytes=60 << 20),
        cost_estimate=pl.CostEstimate(
            flops=6 * rows * features * hidden * count,
            bytes_accessed=6 * (rows + features) * hidden * count,
            transcendentals=0,
        ),
        name="weight_grads",
    )(me, ht, gt, uw, gab, *tokens)


def swap(x, axis, bit):
    return lax.ppermute(x, axis, [(i, i ^ bit) for i in range(lax.axis_size(axis))])


def plane_bits(turn):
    wide = [("fsdp", 1 << b) for b in reversed(range(lax.axis_size("fsdp").bit_length() - 1))]
    near = [("ctx", 1 << b) for b in reversed(range(1, lax.axis_size("ctx").bit_length() - 1))]
    return wide + near if turn == 0 else near + wide


def join(xs, ys):
    out = lax.optimization_barrier((*xs, *ys))
    return list(out[: len(xs)]), list(out[len(xs) :])


def natural(x):
    return with_layout_constraint(x, Layout(major_to_minor=tuple(range(x.ndim))))


def place_of(axis, bit):
    return bit * lax.axis_size("ctx") if axis == "fsdp" else bit


def gather_own(x, turn):
    return [swap(x, axis, bit) for axis, bit in plane_bits(turn)]


def gather_plane(x, own, turn):
    slots = {0: x}
    for (axis, bit), first in zip(plane_bits(turn), own):
        place = place_of(axis, bit)
        slots.update({k + place: swap(v, axis, bit) if k else first for k, v in slots.items()})
    return slots


def gather_near(slots):
    slots = {**slots, **{k + 1: swap(v, "ctx", 1) for k, v in slots.items()}}
    count = len(slots)
    group = max(1, count // 8)
    return [jnp.stack([slots[j + s] for s in range(group)]) for j in range(0, count, group)]


def slot_order(turn):
    order = [0]
    for axis, bit in plane_bits(turn)[::-1]:
        place = place_of(axis, bit)
        order = order + [k + place for k in order]
    return order


def add_up(parts):
    return sum(p.astype(F32) for p in parts)


def scatter_steps(keep, send, turn):
    parts = [keep, swap(send, "ctx", 1)]
    for axis, bit in plane_bits(turn):
        half = parts[0].shape[0] // 2
        total = yield add_up([p[half:] for p in parts]).astype(BF16)
        parts = [p[:half] for p in parts] + [swap(total, axis, bit)]
    yield parts


def tp_shift(x, by):
    n = lax.axis_size("tp")
    return natural(lax.ppermute(natural(x), "tp", [(i, (i + by) % n) for i in range(n)]))


def shifts_tp(x):
    return [x] + [tp_shift(x, by) for by in range(1, lax.axis_size("tp"))]


def order_tp(parts):
    n, i = lax.axis_size("tp"), lax.axis_index("tp")
    return [natural(lax.select_n((i - j) % n, *parts)) for j in range(n)]


def gather_tp(x):
    return jnp.stack(order_tp(shifts_tp(x)))


def scatter_tp(x):
    n, i = lax.axis_size("tp"), lax.axis_index("tp")
    parts = x.reshape(n, -1, x.shape[-1])
    row = lambda k: natural(lax.dynamic_index_in_dim(parts, k % n, 0, keepdims=False))
    return [row(i)] + [tp_shift(row(i + by), by) for by in range(1, n)]


def norm_back(scaled, inverse, gain, upstream):
    weighted = upstream * gain
    gain_part = jnp.sum(upstream * scaled, axis=0)
    return inverse * (weighted - scaled * jnp.mean(weighted * scaled, axis=-1, keepdims=True)), gain_part


def local(
    tokens,
    segment_ids,
    routes,
    gain_first,
    query_weight,
    key_weight,
    value_weight,
    out_weight,
    gain_second,
    router_weight,
    gate_weight,
    up_weight,
    down_weight,
    cotangent,
):
    sequences, width, features = tokens.shape
    rows = sequences * width
    n_ctx = lax.axis_size("ctx")
    q_cols, kv_cols = query_weight.shape[1], key_weight.shape[1]
    repeat = q_cols // kv_cols

    hidden = gate_weight.shape[2]
    shards = lax.axis_size("fsdp") * n_ctx
    me = lax.axis_index("fsdp") * n_ctx + lax.axis_index("ctx")
    me_array = me.astype(jnp.int32).reshape(1)
    first_pack = jnp.concatenate(
        [query_weight, key_weight, value_weight, router_weight, gain_first[:, None], gain_second[:, None]],
        axis=1,
    )
    out_rows = jnp.concatenate(order_tp(shifts_tp(out_weight)), axis=1)
    first_full = lax.all_gather(first_pack, PLANE, axis=0, tiled=True)
    size = EXPERTS // CHUNKS
    packs = [
        jnp.stack([w[at : at + size // 2] for w in (gate_weight, up_weight, down_weight)])
        for at in range(0, EXPERTS, size // 2)
    ]
    own = [gather_own(packs[n], n) for n in range(2)]
    [first_full], [out_rows, *firsts] = join([first_full], [out_rows] + [own[n][0] for n in range(2)])
    edges = (q_cols, q_cols + kv_cols, q_cols + 2 * kv_cols, 2 * q_cols + 2 * kv_cols)
    qkv_full = first_full[:, : edges[2]]
    router_full = first_full[:, edges[2] : -2]
    first_scale = first_full[:, -2].astype(F32)
    second_scale = first_full[:, -1].astype(F32)
    out_full = lax.all_gather(out_rows, PLANE, axis=0, tiled=True)

    flat = natural(tokens.reshape(rows, features)).astype(F32)
    inverse_first = lax.rsqrt(jnp.mean(flat * flat, axis=-1, keepdims=True) + EPSILON)
    scaled_first = flat * inverse_first
    h1 = (scaled_first * first_scale).astype(BF16)
    qkv_t = lax.dot_general(qkv_full, h1, (((0,), (1,)), ((), ())), preferred_element_type=F32).astype(BF16)
    local_heads = q_cols // HD
    q_t = qkv_t[:q_cols].reshape(local_heads, HD, rows)
    k_t = jnp.repeat(qkv_t[q_cols : q_cols + kv_cols].reshape(-1, HD, rows), repeat, axis=0)
    v_t = jnp.repeat(qkv_t[q_cols + kv_cols :].reshape(-1, HD, rows), repeat, axis=0)
    labels = jnp.broadcast_to(segment_ids.reshape(1, 1, rows).astype(BF16), (n_ctx, 16, rows))
    packet = jnp.concatenate([q_t, k_t, v_t, labels], axis=1)
    packet = lax.all_to_all(packet, "ctx", 0, 0, tiled=True)
    segments = packet[:, 3 * HD, :].reshape(1, -1)
    ends = [jnp.sum((segments < k).astype(jnp.int32), axis=1, keepdims=True) for k in (1, 2)]
    starts = jnp.where(segments >= 2, ends[1], jnp.where(segments >= 1, ends[0], 0))
    result_t, lse = attend(packet, starts)
    [result_t], rest = join([result_t], [x for n in range(2) for x in own[n][1:]])
    many = len(rest) // 2
    own = [[firsts[n]] + rest[n * many : (n + 1) * many] for n in range(2)]
    attended_t = lax.all_to_all(result_t, "ctx", 0, 0, tiled=True).reshape(q_cols, rows)
    g = natural(cotangent.reshape(rows, features))
    waiting = own[0] + own[1] + packs[2:] + [g, g.T, out_full]
    [attended_t], waiting = join([attended_t], waiting)
    own, waiting = [waiting[: many + 1], waiting[many + 1 : 2 * many + 2]], waiting[2 * many + 2 :]
    packs[2:], (g, g_t, out_full) = waiting[:2], waiting[2:]
    out_own = lax.dynamic_slice_in_dim(out_full, lax.axis_index("tp") * q_cols, q_cols, axis=1)
    own += [gather_own(packs[2 + n], n) for n in range(2)]
    gathered = [gather_plane(packs[n], own[n], n) for n in range(2)]
    attended_full = lax.all_gather(attended_t, "tp", axis=0, tiled=True)

    def joined(x, n):
        keys = [(m, k) for m in (n, n + 1) for k in gathered[m]]
        [x], slots = join([x], [gathered[m][k] for m, k in keys])
        for (m, k), v in zip(keys, slots):
            gathered[m][k] = v
        return x

    attended_full = joined(attended_full, 0)
    [attended_full], firsts = join([attended_full], [own[2][0], own[3][0]])
    middle = flat + natural(
        lax.dot_general(attended_full, out_full, (((0,), (1,)), ((), ())), preferred_element_type=F32)
    )

    inverse_second = lax.rsqrt(jnp.mean(middle * middle, axis=-1, keepdims=True) + EPSILON)
    scaled_second = middle * inverse_second
    h2 = (scaled_second * second_scale).astype(BF16)
    route_rows = routes.reshape(rows, -1)
    member = jnp.any(route_rows[:, :, None] == jnp.arange(EXPERTS, dtype=jnp.int32)[None, None, :], axis=1)
    logits = jnp.where(member, mm(h2, router_full), -1e30)
    powers = jnp.where(member, jnp.exp(logits - jnp.max(logits, axis=1, keepdims=True)), 0.0)
    gates = powers / jnp.sum(powers, axis=1, keepdims=True)
    [h2], rest = join([h2], own[2][1:] + own[3][1:])
    gathered += [gather_plane(packs[2 + n], [firsts[n]] + rest[n * many : (n + 1) * many], n) for n in range(2)]
    h2_t = h2.T
    grads_of = functools.partial(weight_grads, me_array, h2_t, g_t, shards=shards, hidden=hidden, parts=2)
    weights = gather_near(gathered[0]) + gather_near(gathered[1])
    sums, uw0, gab0 = experts(0, me_array, h2, g, gates, (), weights, F32, ())
    uw0 = joined(uw0, 2)
    weights = gather_near(gathered[2]) + gather_near(gathered[3])
    halves = [grads_of(uw=uw0, gab=gab0, part=0, turn=0, tokens=())]
    [gab0], weights = join([gab0], weights)
    halves.append(grads_of(uw=uw0, gab=gab0, part=1, turn=1, tokens=[halves[0][0]]))
    (expert_sum, ge, dg), uw1, gab1 = experts(
        size, me_array, h2, g, gates, sums, weights, BF16, [keep for keep, _ in halves]
    )
    scatters = [scatter_steps(*halves[n], n) for n in range(2)]
    sends = [next(x) for x in scatters]
    sends = [x.send(y) for x, y in zip(scatters, sends)]
    folded = rows * EXPERTS // features
    both = lax.psum(jnp.concatenate([ge, dg.astype(BF16).reshape(folded, features)], axis=0), "tp")
    [both], sends = join([both], sends)
    ge = both[:rows].astype(F32)
    dg = both[rows:].reshape(rows, EXPERTS).astype(F32)
    dl = (gates * (dg - jnp.sum(gates * dg, axis=1, keepdims=True))).astype(BF16)
    router_part = mm_tn(h2, dl)
    gh2 = ge + mm_nt(dl, router_full)
    middle_part, second_part = norm_back(scaled_second, inverse_second, second_scale, gh2)
    gm = g.astype(F32) + middle_part

    gmr = gm.astype(BF16)
    out_part = lax.dot_general(gmr, attended_t, (((0,), (1,)), ((), ())), preferred_element_type=F32)
    gat_t = lax.dot_general(out_own, gmr, (((0,), (1,)), ((), ())), preferred_element_type=F32).astype(BF16)
    [gat_t], [expert_sum] = join([gat_t], [expert_sum])
    expert_parts = scatter_tp(expert_sum)
    head_grads = lax.all_to_all(gat_t.reshape(local_heads, HD, rows), "ctx", 0, 0, tiled=True)
    halves.append(grads_of(uw=uw1, gab=gab1, part=0, turn=0, tokens=[gat_t]))
    packed_grads = attend_back(packet, head_grads, starts, lse, [halves[2][0]])
    scatters.append(scatter_steps(*halves[2], 0))
    for n in range(2):
        while not isinstance(sends[n], list):
            sends[n] = scatters[n].send(sends[n])
    count = len(sends[0])
    [packed_grads], rest = join([packed_grads], [next(scatters[2]), *sends[0], *sends[1], *expert_parts])
    total, sends, expert_parts = rest[0], [rest[1 : count + 1], rest[count + 1 : 2 * count + 1]], rest[2 * count + 1 :]
    expert_parts = shifts_tp(add_up(expert_parts).astype(BF16))
    halves.append(grads_of(uw=uw1, gab=gab1, part=1, turn=1, tokens=[packed_grads]))
    token_grads = lax.all_to_all(packed_grads, "ctx", 0, 0, tiled=True)
    scatters.append(scatter_steps(*halves[3], 1))
    [token_grads], [last] = join([token_grads], [next(scatters[3])])
    sends += [scatters[2].send(total), scatters[3].send(last)]
    kv_sum = jnp.sum(token_grads[:, HD:].astype(F32).reshape(-1, repeat, 2, HD, rows), axis=1).astype(BF16)
    grads_t = jnp.concatenate(
        [
            token_grads[:, :HD].reshape(q_cols, rows),
            kv_sum[:, 0].reshape(kv_cols, rows),
            kv_sum[:, 1].reshape(kv_cols, rows),
        ],
        axis=0,
    )
    gh1 = lax.dot_general(grads_t, qkv_full, (((0,), (1,)), ((), ())), preferred_element_type=F32)
    first_part = jnp.sum(gh1 * scaled_first, axis=0)
    gh1 = add_up(scatter_tp(natural(gh1.astype(BF16)))).astype(BF16)
    first_part = jnp.sum(gather_tp(first_part[None, :]), axis=0)
    qkv_part = lax.dot_general(h1, grads_t, (((0,), (1,)), ((), ())), preferred_element_type=F32)
    thin_part = jnp.concatenate(
        [router_part, first_part.T, second_part[:, None], jnp.zeros((features, 128 - EXPERTS - 2), F32)], axis=1
    )
    wide = natural(jnp.concatenate([natural(x.astype(BF16)) for x in (qkv_part, out_part, thin_part)], axis=1))
    [gh1], [wide, *rest] = join([gh1], [wide, *sends[2:], *expert_parts])
    sends[2:], expert_parts = rest[:2], rest[2:]
    expert_total = natural(jnp.concatenate(order_tp(expert_parts), axis=0))
    output = natural((middle + expert_total.astype(F32)).astype(BF16)).reshape(tokens.shape)
    wide = lax.psum_scatter(wide, PLANE, scatter_dimension=0, tiled=True).astype(F32)
    gh1 = natural(jnp.concatenate(order_tp(shifts_tp(natural(gh1))), axis=0)).astype(F32)
    for n in range(4):
        while not isinstance(sends[n], list):
            sends[n] = scatters[n].send(sends[n])
    gate_grad, up_grad, down_grad = (
        jnp.concatenate([add_up([x[0, t] for x in parts]) for parts in sends], axis=0) for t in range(3)
    )
    token_part, _ = norm_back(scaled_first, inverse_first, first_scale, gh1)
    input_grad = natural(gm + token_part).reshape(tokens.shape)
    return (
        output,
        input_grad,
        wide[:, edges[3] + EXPERTS],
        wide[:, : edges[0]],
        wide[:, edges[0] : edges[1]],
        wide[:, edges[1] : edges[2]],
        wide[:, edges[2] : edges[3]],
        wide[:, edges[3] + EXPERTS + 1],
        wide[:, edges[3] : edges[3] + EXPERTS],
        gate_grad,
        up_grad,
        down_grad,
    )


def solution(mesh):
    return jax.shard_map(
        local,
        mesh=mesh,
        in_specs=(
            P("fsdp", "ctx", None),
            P("fsdp", "ctx"),
            P("fsdp", "ctx", None),
            P(PLANE),
            P(PLANE, "tp"),
            P(PLANE, "tp"),
            P(PLANE, "tp"),
            P(PLANE, "tp"),
            P(PLANE),
            P(PLANE, None),
            P(None, PLANE, "tp"),
            P(None, PLANE, "tp"),
            P(None, PLANE, "tp"),
            P("fsdp", "ctx", None),
        ),
        out_specs=(
            P("fsdp", "ctx", None),
            P("fsdp", "ctx", None),
            P(PLANE),
            P(PLANE, "tp"),
            P(PLANE, "tp"),
            P(PLANE, "tp"),
            P(PLANE, "tp"),
            P(PLANE),
            P(PLANE, None),
            P(None, PLANE, "tp"),
            P(None, PLANE, "tp"),
            P(None, PLANE, "tp"),
        ),
        check_vma=False,
    )
```
